256 devices in a mesh: req: 4 (over x), cand: 64 (over y, z, core).
Axes of the slice: x: 4, y: 4, z: 8, core: 2. Of those that a mesh axis runs over, the one named last changes fastest.
Arguments:
- cand_emb: bfloat16 [131072, 512], P(('req', 'cand')), may hold values from -6 to 6
- cand_req: int32 [131072], P(('req', 'cand')), may hold values from 0 to 31, as said below
- expert_ids: int32 [131072], P(('req', 'cand')), may hold values from 0 to 63, as said below
- user_state: bfloat16 [1024, 512], P(('req', 'cand')), may hold values from -6 to 6
- d_out: bfloat16 [131072, 512], P(('req', 'cand')), may hold values from -6 to 6
- w_in: bfloat16 [64, 512, 2048], P('cand'), may hold values from -0.25 to 0.25
- w_out: bfloat16 [64, 2048, 512], P('cand'), may hold values from -0.125 to 0.125
Outputs:
- tower_out: bfloat16 [131072, 512], P(('req', 'cand'))
- cand_grad: bfloat16 [131072, 512], P(('req', 'cand'))
- user_grad: float32 [1024, 512], P(('req', 'cand'))
The draws below stay inside these ranges and needn't reach their ends.
Inputs may be any that keep to these rules, and one draw needn't show every extreme that they name: `cand_req`: candidates on devices with req index g name requests g * 8 to g * 8 + 7. `expert_ids`: in each device's aligned block of 512 rows no expert is named by more than 16 rows; on the devices of one req index one expert is named exactly 16 times in every block.
All inputs are finite; a program needn't handle non-finite values.
Results may differ from the reference program's by a relative error of at most 0.0076.
Values may be sent and summed in bfloat16 or wider, within the bound.
No kernel may reach another device: no remote copies, remote signals or barrier semaphores. Data moves between devices by JAX's collectives and lax.ppermute only.
A program may use at most 64 MiB of HBM per device.

```python
import math
import jax
import jax.numpy as jnp
from jax import lax

D = 512
FF = 2048
US = 32
CAND_DEV = 512
REQ_DEV = 8
EXPERTS = 64
CAP = 16
REQ = 32
GROUP_ROWS = 256
USER_ROWS = 1024
GROUP_CANDS = 32768
NC = 131072
N_REQ = 4


def draw_user_state(key, part):
    key = jax.random.fold_in(key, 5)
    values = jax.random.normal(key, (USER_ROWS, D), jnp.float32)
    return jnp.clip(values, -6.0, 6.0).astype(jnp.bfloat16)


def draw_cand_emb(key, part):
    key = jax.random.fold_in(key, 7)
    values = jax.random.normal(key, (NC, D), jnp.float32)
    return jnp.clip(values, -6.0, 6.0).astype(jnp.bfloat16)


def draw_cand_req(key, part):
    key = jax.random.fold_in(key, 9)
    group = jnp.arange(NC, dtype=jnp.int32) // GROUP_CANDS
    return group * REQ_DEV + jax.random.randint(key, (NC,), 0, REQ_DEV, dtype=jnp.int32)


def draw_expert_ids(key, part):
    key = jax.random.fold_in(key, 11)
    block_count = NC // CAND_DEV
    group_count = REQ // REQ_DEV
    hot_experts = jax.random.randint(jax.random.fold_in(key, 1), (group_count,), 0, EXPERTS, dtype=jnp.int32)
    block_hot = jnp.repeat(hot_experts, block_count // group_count)
    block_keys = jax.random.split(jax.random.fold_in(key, 2), block_count)

    def one_block(block_key, hot_one):
        first, second = jax.random.split(block_key)
        picked = jax.random.permutation(first, (EXPERTS - 1) * CAP)[:CAND_DEV - CAP].astype(jnp.int32)
        others = (hot_one + 1 + picked // CAP) % EXPERTS
        entries = jnp.concatenate([jnp.full((CAP,), hot_one, jnp.int32), others])
        return jax.random.permutation(second, entries)
    return jax.vmap(one_block)(block_keys, block_hot).reshape(NC).astype(jnp.int32)


def steps_of(stream_key, shape, pieces, low, high):
    gain, own = 1.0, jax.random.fold_in(stream_key, 6)
    for dim, blocks in pieces:
        draws = jnp.exp(jax.random.uniform(jax.random.fold_in(own, dim), (blocks,), jnp.float32, low / len(pieces), high / len(pieces)))
        gain = gain * jnp.repeat(draws, shape[dim] // blocks).reshape([-1 if axis == dim else 1 for axis in range(len(shape))])
    return gain


def bell_draw(rng, extent, width, bound, pieces=(), held_as=jnp.bfloat16):
    loudness = steps_of(rng, extent, pieces, -0.22, 0.18) if pieces else 1.0
    values = jax.random.normal(rng, extent, jnp.float32) * width * loudness
    return jnp.minimum(jnp.maximum(values, -bound), bound).astype(held_as)


def setup_inputs(seed: int = 0) -> dict:
    splits = jax.random.split(jax.random.key(seed), 8)
    return {
        "cand_emb": draw_cand_emb(jax.random.fold_in(splits[7], 71), 0),
        "cand_req": draw_cand_req(jax.random.fold_in(splits[7], 71), 0),
        "expert_ids": draw_expert_ids(jax.random.fold_in(splits[7], 71), 0),
        "user_state": draw_user_state(jax.random.fold_in(splits[7], 71), 0),
        "d_out": bell_draw(splits[4], (NC, D), 1.0, 6.0, ((0, 256),)),
        "w_in": bell_draw(splits[5], (EXPERTS, D, FF), D ** -0.5, 0.25, ((0, 64),)),
        "w_out": bell_draw(splits[6], (EXPERTS, FF, D), FF ** -0.5, 0.125, ((0, 64),)),
    }


def attend(queries, keys, local_req):
    scale = 1.0 / math.sqrt(D)
    scores = jnp.dot(queries, keys.T, preferred_element_type=jnp.float32) * scale
    member = local_req[:, None] == (jnp.arange(keys.shape[0], dtype=jnp.int32) // US)[None, :]
    peak = lax.optimization_barrier(jnp.max(jnp.where(member, scores, -jnp.inf), axis=1, keepdims=True))
    weights = jnp.exp(jnp.where(member, scores - peak, -jnp.inf))
    return weights / lax.optimization_barrier(jnp.sum(weights, axis=1, keepdims=True))

def expert_pass(inputs, grads, expert_ids, w_in, w_out):
    limit = NC // CAND_DEV * CAP
    pad_in = jnp.concatenate([inputs, jnp.zeros((1, D), jnp.bfloat16)], axis=0)
    pad_grad = jnp.concatenate([grads, jnp.zeros((1, D), jnp.bfloat16)], axis=0)
    outputs = jnp.zeros((NC + 1, D), jnp.bfloat16)
    back_in = jnp.zeros((NC + 1, D), jnp.bfloat16)

    def step(expert, carry):
        outputs, back_in = carry
        index = jnp.nonzero(expert_ids == expert, size=limit, fill_value=NC)[0].astype(jnp.int32)
        rows_in = pad_in[index].astype(jnp.float32)
        rows_grad = pad_grad[index].astype(jnp.float32)
        first = w_in[expert].astype(jnp.float32)
        second = w_out[expert].astype(jnp.float32)
        pre = jnp.dot(rows_in, first)
        hidden = jax.nn.gelu(pre).astype(jnp.bfloat16)
        result = jnp.dot(hidden.astype(jnp.float32), second).astype(jnp.bfloat16)
        back = jnp.dot(rows_grad, second.T)
        activated, pull_back = jax.vjp(jax.nn.gelu, pre)
        d_pre = pull_back(back)[0].astype(jnp.bfloat16)
        d_in = jnp.dot(d_pre.astype(jnp.float32), first.T).astype(jnp.bfloat16)
        return (outputs.at[index].set(result), back_in.at[index].set(d_in))
    outputs, back_in = lax.fori_loop(0, EXPERTS, step, (outputs, back_in))
    return (outputs[:NC], back_in[:NC])

def reference(cand_emb, cand_req, expert_ids, user_state, d_out, w_in, w_out):
    scale = 1.0 / math.sqrt(D)
    input_blocks = []
    prob_blocks = []
    for group in range(N_REQ):
        start = group * GROUP_CANDS
        queries = cand_emb[start:start + GROUP_CANDS]
        keys = user_state[group * GROUP_ROWS:(group + 1) * GROUP_ROWS]
        local_req = cand_req[start:start + GROUP_CANDS] - group * REQ_DEV
        probs = attend(queries, keys, local_req)
        probs_b = probs.astype(jnp.bfloat16)
        mixed = jnp.dot(probs_b, keys, preferred_element_type=jnp.float32)
        input_blocks.append((queries.astype(jnp.float32) + mixed).astype(jnp.bfloat16))
        prob_blocks.append(probs)
    tower_in = jnp.concatenate(input_blocks, axis=0)
    tower_out, d_in = expert_pass(tower_in, d_out, expert_ids, w_in, w_out)
    grad_blocks = []
    user_blocks = []
    for group in range(N_REQ):
        start = group * GROUP_CANDS
        queries = cand_emb[start:start + GROUP_CANDS]
        keys = user_state[group * GROUP_ROWS:(group + 1) * GROUP_ROWS]
        probs = prob_blocks[group]
        probs_b = probs.astype(jnp.bfloat16)
        grad_rows = d_in[start:start + GROUP_CANDS]
        d_probs = jnp.dot(grad_rows, keys.T, preferred_element_type=jnp.float32)
        center = lax.optimization_barrier(jnp.sum(probs * d_probs, axis=1, keepdims=True))
        slope = (probs * (d_probs - center)).astype(jnp.bfloat16)
        cand_part = grad_rows.astype(jnp.float32) + jnp.dot(slope, keys, preferred_element_type=jnp.float32) * scale
        grad_blocks.append(cand_part.astype(jnp.bfloat16))
        user_part = jnp.dot(probs_b.T, grad_rows, preferred_element_type=jnp.float32)
        user_part = user_part + jnp.dot(slope.T, queries, preferred_element_type=jnp.float32) * scale
        user_blocks.append(user_part)
    cand_grad = jnp.concatenate(grad_blocks, axis=0)
    user_grad = jnp.concatenate(user_blocks, axis=0)
    return (tower_out, cand_grad, user_grad)
```

```python
import math

import jax
import jax.numpy as jnp
from jax import lax
from jax.sharding import PartitionSpec as P

US = 32
REQ_DEV = 8


def dot(a, b, dims):
    return lax.dot_general(a, b, (dims, ((), ())), preferred_element_type=jnp.float32)


def exchange(blocks):
    return lax.all_to_all(blocks, "cand", split_axis=0, concat_axis=0, tiled=True)


def shards(cand_emb, cand_req, expert_ids, user_state, d_out, w_in, w_out):
    row_count, width = cand_emb.shape
    scale = 1.0 / math.sqrt(width)
    devices = lax.axis_size("cand")
    experts = devices * w_in.shape[0]
    capacity = 2 * row_count // experts
    slots = experts * capacity
    w_in, w_out = w_in[0], w_out[0]

    keys = exchange(jnp.broadcast_to(user_state[None], (devices,) + user_state.shape))
    keys = keys.reshape(-1, width)

    onehot = (expert_ids[:, None] == jnp.arange(experts, dtype=jnp.int32)[None, :]).astype(jnp.bfloat16)
    rows = jnp.arange(row_count, dtype=jnp.int32)
    below = (rows[:, None] > rows[None, :]).astype(jnp.bfloat16)
    ranks = dot(below, onehot, ((1,), (0,)))
    slot = jnp.sum(onehot.astype(jnp.float32) * ranks, axis=1).astype(jnp.int32)
    place = expert_ids * capacity + slot
    spread = (jnp.arange(slots, dtype=jnp.int32)[:, None] == place[None, :]).astype(jnp.bfloat16)

    def send(values):
        packed = dot(spread, values, ((1,), (0,))).astype(jnp.bfloat16)
        return exchange(packed.reshape(devices, capacity, width)).reshape(slots, width)

    def fetch(values):
        back = exchange(values.reshape(devices, capacity, width)).reshape(slots, width)
        return dot(spread, back, ((0,), (0,))).astype(jnp.bfloat16)

    grads = send(d_out)

    local_req = cand_req - lax.axis_index("req") * REQ_DEV
    scores = dot(cand_emb, keys, ((1,), (1,))) * scale
    member = local_req[:, None] == (jnp.arange(keys.shape[0], dtype=jnp.int32) // US)[None, :]
    peak = jnp.max(jnp.where(member, scores, -jnp.inf), axis=1, keepdims=True)
    weights = jnp.exp(jnp.where(member, scores - peak, -jnp.inf))
    probs = weights / jnp.sum(weights, axis=1, keepdims=True)
    probs_b = probs.astype(jnp.bfloat16)
    tower_in = (cand_emb.astype(jnp.float32) + dot(probs_b, keys, ((1,), (0,)))).astype(jnp.bfloat16)
    inputs = send(tower_in)

    back = dot(grads, w_out, ((1,), (1,)))
    pre = dot(inputs, w_in, ((1,), (0,)))
    activated, pull_back = jax.vjp(jax.nn.gelu, pre)
    d_pre = pull_back(back)[0].astype(jnp.bfloat16)
    d_in = fetch(dot(d_pre, w_in, ((1,), (1,))).astype(jnp.bfloat16))
    hidden = activated.astype(jnp.bfloat16)
    tower_out = fetch(dot(hidden, w_out, ((1,), (0,))).astype(jnp.bfloat16))

    d_probs = dot(d_in, keys, ((1,), (1,)))
    center = jnp.sum(probs * d_probs, axis=1, keepdims=True)
    slope = (probs * (d_probs - center)).astype(jnp.bfloat16)
    share = dot(probs_b, d_in, ((0,), (0,))) + dot(slope, cand_emb, ((0,), (0,))) * scale
    shares = exchange(share.astype(jnp.bfloat16).reshape(devices, -1, width))
    user_grad = jnp.sum(shares.astype(jnp.float32), axis=0)
    cand_grad = (d_in.astype(jnp.float32) + dot(slope, keys, ((1,), (0,))) * scale).astype(jnp.bfloat16)
    return (tower_out, cand_grad, user_grad)


def solution(mesh):
    rows = P(("req", "cand"), None)
    ids = P(("req", "cand"))
    weights = P("cand", None, None)
    in_specs = (rows, ids, ids, rows, rows, weights, weights)
    return jax.shard_map(shards, mesh=mesh, in_specs=in_specs, out_specs=(rows, rows, rows), check_vma=False)
```

```python
import functools
import math

import jax
import jax.numpy as jnp
from jax import lax
from jax.experimental import pallas as pl
from jax.experimental.pallas import tpu as pltpu
from jax.sharding import PartitionSpec as P

US = 32
REQ_DEV = 8
LANES = 128
MIB = 1024 * 1024


def dot(a, b, dims=((1,), (0,))):
    return lax.dot_general(a, b, (dims, ((), ())), preferred_element_type=jnp.float32)


def iota(shape, dim):
    return lax.broadcasted_iota(jnp.int32, shape, dim)


def as_column(row):
    size = row.shape[1]
    eye = iota((size, size), 0) == iota((size, size), 1)
    return jnp.sum(jnp.where(eye, row, 0.0), axis=1, keepdims=True)


def read_rows(ref, first, count, width):
    blocks = ref.shape[0]
    chunks = [
        ref[:, first + c * count : first + (c + 1) * count, :].reshape(blocks * count, LANES)
        for c in range(width // LANES)
    ]
    return jnp.concatenate(chunks, axis=1)


def write_rows(ref, first, count, rows):
    blocks = ref.shape[0]
    for c in range(rows.shape[1] // LANES):
        ref[:, first + c * count : first + (c + 1) * count, :] = rows[:, c * LANES : (c + 1) * LANES].reshape(
            blocks, count, LANES
        )


def pack_kernel(capacity, ids_ref, req_ref, emb_ref, grad_ref, user_ref, send_ref, place_ref):
    experts = send_ref.shape[0]
    count, width = emb_ref.shape
    chunks = width // LANES
    ids = ids_ref[...].astype(jnp.float32)
    named = (iota((experts, count), 0).astype(jnp.float32) == ids).astype(jnp.bfloat16)
    earlier = (iota((count, count), 0) < iota((count, count), 1)).astype(jnp.bfloat16)
    slot = jnp.sum(named.astype(jnp.float32) * dot(named, earlier), axis=0, keepdims=True)
    place = ids * capacity + slot
    place_ref[...] = place
    spread = (iota((experts * capacity, count), 0).astype(jnp.float32) == place).astype(jnp.bfloat16)
    write_rows(send_ref, 0, capacity, dot(spread, emb_ref[...]).astype(jnp.bfloat16))
    write_rows(send_ref, chunks * capacity, capacity, dot(spread, grad_ref[...]).astype(jnp.bfloat16))
    first = 2 * chunks * capacity
    at_slot = iota((count, LANES), 1).astype(jnp.float32) == as_column(slot)
    requests = dot(named, jnp.where(at_slot, as_column(req_ref[...].astype(jnp.float32)), 0.0).astype(jnp.bfloat16))
    own = user_ref.shape[0]
    user = jnp.concatenate([user_ref[:, c * LANES : (c + 1) * LANES] for c in range(chunks)], axis=0)
    tail = send_ref.shape[1] - first
    user_tail = jnp.concatenate(
        [user.astype(jnp.float32), jnp.zeros((tail - chunks * own, LANES), jnp.float32)], axis=0
    )
    is_request = iota((experts, tail, LANES), 1) == chunks * own
    send_ref[:, first:, :] = jnp.where(is_request, requests[:, None, :], user_tail[None]).astype(jnp.bfloat16)


def work_kernel(capacity, own, recv_ref, w_in_ref, w_out_ref, send_ref):
    sources = recv_ref.shape[0]
    width, hidden_width = w_in_ref.shape
    chunks = width // LANES
    count = sources * capacity
    scale = 1.0 / math.sqrt(width)
    emb = read_rows(recv_ref, 0, capacity, width)
    grad = read_rows(recv_ref, chunks * capacity, capacity, width)
    first = 2 * chunks * capacity
    keys_n = sources * own
    user_rows = chunks * own
    flat = recv_ref[:, first : first + user_rows, :].reshape(sources * user_rows, LANES)
    key_of = iota((keys_n, sources * user_rows), 0)
    row_of = iota((keys_n, sources * user_rows), 1)
    keys = jnp.concatenate(
        [
            dot((row_of == key_of // own * user_rows + c * own + key_of % own).astype(jnp.bfloat16), flat)
            for c in range(chunks)
        ],
        axis=1,
    ).astype(jnp.bfloat16)
    requests = recv_ref[:, first + user_rows, :].astype(jnp.bfloat16)
    source_of = (iota((count, sources), 0) // capacity == iota((count, sources), 1)).astype(jnp.bfloat16)
    spread = dot(source_of, requests)
    mine = iota((count, LANES), 1) == iota((count, LANES), 0) % capacity
    request = jnp.sum(jnp.where(mine, spread, 0.0), axis=1, keepdims=True)
    member = (iota((count, keys_n), 1) // US).astype(jnp.float32) == request

    scores = dot(emb, keys, ((1,), (1,))) * scale
    peak = jnp.max(jnp.where(member, scores, -jnp.inf), axis=1, keepdims=True)
    weights = jnp.exp(jnp.where(member, scores - peak, -jnp.inf))
    probs = weights / jnp.sum(weights, axis=1, keepdims=True)
    probs_b = probs.astype(jnp.bfloat16)
    inputs = (emb.astype(jnp.float32) + dot(probs_b, keys)).astype(jnp.bfloat16)

    c0 = math.sqrt(2.0 / math.pi)
    out = jnp.zeros((count, width), jnp.float32)
    back_in = jnp.zeros((count, width), jnp.float32)
    step = 256
    for f in range(0, hidden_width, step):
        first_w = w_in_ref[:, f : f + step]
        second_w = w_out_ref[f : f + step, :]
        pre = dot(inputs, first_w)
        back = dot(grad, second_w, ((1,), (1,)))
        square = pre * pre
        half = 0.5 + 0.5 * jnp.tanh(pre * (c0 + (c0 * 0.044715) * square))
        gelu = pre * half
        slope_g = half + gelu * (1.0 - half) * (2.0 * c0 + (6.0 * c0 * 0.044715) * square)
        out = out + dot(gelu.astype(jnp.bfloat16), second_w)
        back_in = back_in + dot((back * slope_g).astype(jnp.bfloat16), first_w, ((1,), (1,)))
    write_rows(send_ref, 0, capacity, out.astype(jnp.bfloat16))
    d_in = back_in.astype(jnp.bfloat16)

    d_probs = dot(d_in, keys, ((1,), (1,)))
    center = jnp.sum(probs * d_probs, axis=1, keepdims=True)
    slope = (probs * (d_probs - center)).astype(jnp.bfloat16)
    cand_grad = d_in.astype(jnp.float32) + dot(slope, keys) * scale
    write_rows(send_ref, chunks * capacity, capacity, cand_grad.astype(jnp.bfloat16))
    share = dot(probs_b, d_in, ((0,), (0,))) + dot(slope, emb, ((0,), (0,))) * scale
    share = share.astype(jnp.bfloat16)
    place_of = iota((sources * user_rows, keys_n), 0)
    from_key = iota((sources * user_rows, keys_n), 1)
    tail = jnp.zeros((sources * user_rows, LANES), jnp.float32)
    for c in range(chunks):
        pick = place_of == from_key // own * user_rows + c * own + from_key % own
        tail = tail + dot(pick.astype(jnp.bfloat16), share[:, c * LANES : (c + 1) * LANES])
    send_ref[:, first : first + user_rows, :] = tail.reshape(sources, user_rows, LANES).astype(jnp.bfloat16)


def unpack_kernel(capacity, own, recv_ref, place_ref, out_ref, grad_ref, user_ref):
    experts = recv_ref.shape[0]
    count, width = out_ref.shape
    chunks = width // LANES
    place = as_column(place_ref[...])
    pick = (iota((count, experts * capacity), 1).astype(jnp.float32) == place).astype(jnp.bfloat16)
    out_ref[...] = dot(pick, read_rows(recv_ref, 0, capacity, width)).astype(jnp.bfloat16)
    grad_ref[...] = dot(pick, read_rows(recv_ref, chunks * capacity, capacity, width)).astype(jnp.bfloat16)
    first = 2 * chunks * capacity
    total = jnp.sum(recv_ref[:, first:, :].astype(jnp.float32), axis=0)
    for c in range(chunks):
        user_ref[:, c * LANES : (c + 1) * LANES] = total[c * own : (c + 1) * own, :]


def exchange(blocks):
    return lax.all_to_all(blocks, "cand", split_axis=0, concat_axis=0, tiled=True)


def shards(cand_emb, cand_req, expert_ids, user_state, d_out, w_in, w_out):
    count, width = cand_emb.shape
    own = user_state.shape[0]
    experts = lax.axis_size("cand") * w_in.shape[0]
    capacity = 2 * count // experts
    chunks = width // LANES
    body = chunks * (2 * capacity + own)
    there = body + 8
    local_req = cand_req - lax.axis_index("req") * REQ_DEV
    send, place = pl.pallas_call(
        functools.partial(pack_kernel, capacity),
        out_shape=(
            jax.ShapeDtypeStruct((experts, there, LANES), jnp.bfloat16),
            jax.ShapeDtypeStruct((1, count), jnp.float32),
        ),
        compiler_params=pltpu.CompilerParams(vmem_limit_bytes=24 * MIB),
        name="pack",
    )(expert_ids[None], local_req[None], cand_emb, d_out, user_state)
    recv = exchange(send)
    send = pl.pallas_call(
        functools.partial(work_kernel, capacity, own),
        out_shape=jax.ShapeDtypeStruct((experts, body, LANES), jnp.bfloat16),
        scratch_shapes=[],
        compiler_params=pltpu.CompilerParams(vmem_limit_bytes=56 * MIB),
        name="work",
    )(recv, w_in[0], w_out[0])
    recv = exchange(send)
    tower_out, cand_grad, user_grad = pl.pallas_call(
        functools.partial(unpack_kernel, capacity, own),
        out_shape=(
            jax.ShapeDtypeStruct((count, width), jnp.bfloat16),
            jax.ShapeDtypeStruct((count, width), jnp.bfloat16),
            jax.ShapeDtypeStruct((own, width), jnp.float32),
        ),
        compiler_params=pltpu.CompilerParams(vmem_limit_bytes=24 * MIB),
        name="unpack",
    )(recv, place)
    return (tower_out, cand_grad, user_grad)


def solution(mesh):
    rows = P(("req", "cand"), None)
    ids = P(("req", "cand"))
    weights = P("cand", None, None)
    in_specs = (rows, ids, ids, rows, rows, weights, weights)
    return jax.shard_map(shards, mesh=mesh, in_specs=in_specs, out_specs=(rows, rows, rows), check_vma=False)
```

```python
import functools
import math

import jax
import jax.numpy as jnp
from jax import lax
from jax.experimental import pallas as pl
from jax.experimental.pallas import tpu as pltpu
from jax.sharding import PartitionSpec as P

US = 32
REQ_DEV = 8
LANES = 128
MIB = 1024 * 1024


def dot(a, b, dims=((1,), (0,))):
    return lax.dot_general(a, b, (dims, ((), ())), preferred_element_type=jnp.float32)


def iota(shape, dim):
    return lax.broadcasted_iota(jnp.int32, shape, dim)


def as_column(row):
    size = row.shape[1]
    eye = iota((size, size), 0) == iota((size, size), 1)
    return jnp.sum(jnp.where(eye, row, 0.0), axis=1, keepdims=True)


def read_rows(ref, first, count, width):
    blocks = ref.shape[0]
    chunks = [
        ref[:, first + c * count : first + (c + 1) * count, :].reshape(blocks * count, LANES)
        for c in range(width // LANES)
    ]
    return jnp.concatenate(chunks, axis=1)


def write_rows(ref, first, count, rows):
    blocks = ref.shape[0]
    for c in range(rows.shape[1] // LANES):
        ref[:, first + c * count : first + (c + 1) * count, :] = rows[:, c * LANES : (c + 1) * LANES].reshape(
            blocks, count, LANES
        )


def pack_kernel(
    capacity, ids_hbm, req_hbm, emb_hbm, grad_hbm, user_hbm, send_hbm, place_ref,
    ids_ref, req_ref, emb_ref, grad_ref, user_ref, send_ref, sems, out_sems,
):
    pairs = (
        (ids_hbm, ids_ref), (req_hbm, req_ref), (user_hbm, user_ref), (emb_hbm, emb_ref), (grad_hbm, grad_ref),
    )
    copies = [pltpu.make_async_copy(src, dst, sems.at[i]) for i, (src, dst) in enumerate(pairs)]
    for copy in copies:
        copy.start()
    experts = send_ref.shape[0]
    count, width = emb_ref.shape
    chunks = width // LANES
    own = user_ref.shape[0]
    earlier = (iota((count, count), 0) < iota((count, count), 1)).astype(jnp.bfloat16)
    copies[0].wait()
    ids = ids_ref[...].astype(jnp.float32)
    named = (iota((experts, count), 0).astype(jnp.float32) == ids).astype(jnp.bfloat16)
    slot = jnp.sum(named.astype(jnp.float32) * dot(named, earlier), axis=0, keepdims=True)
    place = ids * capacity + slot
    place_ref[...] = place
    copies[1].wait()
    copies[2].wait()
    first = 2 * chunks * capacity
    local_req = (req_ref[...] & (REQ_DEV - 1)).astype(jnp.float32)
    at_slot = iota((count, LANES), 1).astype(jnp.float32) == as_column(slot)
    requests = dot(named, jnp.where(at_slot, as_column(local_req), 0.0).astype(jnp.bfloat16))
    user = jnp.concatenate([user_ref[:, c * LANES : (c + 1) * LANES] for c in range(chunks)], axis=0)
    tail = send_ref.shape[1] - first
    user_tail = jnp.concatenate(
        [user.astype(jnp.float32), jnp.zeros((tail - chunks * own, LANES), jnp.float32)], axis=0
    )
    is_request = iota((experts, tail, LANES), 1) == chunks * own
    send_ref[:, first:, :] = jnp.where(is_request, requests[:, None, :], user_tail[None]).astype(jnp.bfloat16)
    copies[3].wait()
    copies[4].wait()
    parts = out_sems.shape[0]
    blocks = experts // parts
    slot_of = iota((blocks * capacity, count), 0).astype(jnp.float32)
    outs = []
    for p in range(parts):
        spread = (slot_of == place - float(p * blocks * capacity)).astype(jnp.bfloat16)
        part = send_ref.at[p * blocks : (p + 1) * blocks]
        write_rows(part, 0, capacity, dot(spread, emb_ref[...]).astype(jnp.bfloat16))
        write_rows(part, chunks * capacity, capacity, dot(spread, grad_ref[...]).astype(jnp.bfloat16))
        outs.append(pltpu.make_async_copy(part, send_hbm.at[p * blocks : (p + 1) * blocks], out_sems.at[p]))
        outs[p].start()
    for copy in outs:
        copy.wait()


def work_kernel(capacity, own, recv_ref, w_in_ref, w_out_ref, send_ref):
    sources = recv_ref.shape[0]
    width = w_in_ref.shape[0]
    chunks = width // LANES
    count = sources * capacity
    scale = 1.0 / math.sqrt(width)
    emb = read_rows(recv_ref, 0, capacity, width)
    grad = read_rows(recv_ref, chunks * capacity, capacity, width)
    first = 2 * chunks * capacity
    keys_n = sources * own
    user_rows = chunks * own
    users = recv_ref[:, first : first + user_rows, :].astype(jnp.float32)
    keys = jnp.concatenate(
        [users[:, c * own : (c + 1) * own, :].reshape(keys_n, LANES) for c in range(chunks)], axis=1
    ).astype(jnp.bfloat16)
    requests = recv_ref[:, first + user_rows, :].astype(jnp.bfloat16)
    source_of = (iota((count, sources), 0) // capacity == iota((count, sources), 1)).astype(jnp.bfloat16)
    spread = dot(source_of, requests)
    mine = iota((count, LANES), 1) == iota((count, LANES), 0) % capacity
    request = jnp.sum(jnp.where(mine, spread, 0.0), axis=1, keepdims=True)
    member = (iota((count, keys_n), 1) // US).astype(jnp.float32) == request

    scores = dot(emb, keys, ((1,), (1,))) * scale
    peak = jnp.max(jnp.where(member, scores, -jnp.inf), axis=1, keepdims=True)
    weights = jnp.exp(jnp.where(member, scores - peak, -jnp.inf))
    probs = weights / jnp.sum(weights, axis=1, keepdims=True)
    probs_b = probs.astype(jnp.bfloat16)
    inputs = (emb.astype(jnp.float32) + dot(probs_b, keys)).astype(jnp.bfloat16)

    c0 = math.sqrt(2.0 / math.pi)
    outs, backs = [], []
    tile = count // 4
    for m in range(0, count, tile):
        pre = dot(inputs[m : m + tile], w_in_ref[...])
        back = dot(grad[m : m + tile], w_out_ref[...], ((1,), (1,)))
        square = pre * pre
        half = 0.5 + 0.5 * jnp.tanh(pre * (c0 + (c0 * 0.044715) * square))
        gelu = pre * half
        slope_g = half + gelu * (1.0 - half) * (2.0 * c0 + (6.0 * c0 * 0.044715) * square)
        outs.append(dot(gelu.astype(jnp.bfloat16), w_out_ref[...]).astype(jnp.bfloat16))
        backs.append(dot((back * slope_g).astype(jnp.bfloat16), w_in_ref[...], ((1,), (1,))).astype(jnp.bfloat16))
    write_rows(send_ref, 0, capacity, jnp.concatenate(outs, axis=0))
    d_in = jnp.concatenate(backs, axis=0)

    d_probs = dot(d_in, keys, ((1,), (1,)))
    center = jnp.sum(probs * d_probs, axis=1, keepdims=True)
    slope = (probs * (d_probs - center)).astype(jnp.bfloat16)
    cand_grad = d_in.astype(jnp.float32) + dot(slope, keys) * scale
    write_rows(send_ref, chunks * capacity, capacity, cand_grad.astype(jnp.bfloat16))
    share = dot(probs_b, d_in, ((0,), (0,))) + dot(slope, emb, ((0,), (0,))) * scale
    tail = jnp.concatenate(
        [share[:, c * LANES : (c + 1) * LANES].reshape(sources, own, LANES) for c in range(chunks)], axis=1
    )
    send_ref[:, first : first + user_rows, :] = tail.astype(jnp.bfloat16)


def unpack_kernel(capacity, own, recv_ref, place_ref, out_hbm, grad_hbm, user_hbm, out_ref, grad_ref, user_ref, sems):
    experts = recv_ref.shape[0]
    count, width = out_ref.shape
    chunks = width // LANES
    first = 2 * chunks * capacity
    total = jnp.sum(recv_ref[:, first:, :].astype(jnp.float32), axis=0)
    for c in range(chunks):
        user_ref[:, c * LANES : (c + 1) * LANES] = total[c * own : (c + 1) * own, :]
    copies = [pltpu.make_async_copy(user_ref, user_hbm, sems.at[0])]
    copies[0].start()
    place = as_column(place_ref[...])
    pick = (iota((count, experts * capacity), 1).astype(jnp.float32) == place).astype(jnp.bfloat16)
    out_ref[...] = dot(pick, read_rows(recv_ref, 0, capacity, width)).astype(jnp.bfloat16)
    copies.append(pltpu.make_async_copy(out_ref, out_hbm, sems.at[1]))
    copies[1].start()
    grads = read_rows(recv_ref, chunks * capacity, capacity, width)
    part = count // 2
    for p in range(2):
        rows = pl.ds(p * part, part)
        grad_ref[rows, :] = dot(pick[p * part : (p + 1) * part], grads).astype(jnp.bfloat16)
        copies.append(pltpu.make_async_copy(grad_ref.at[rows, :], grad_hbm.at[rows, :], sems.at[2 + p]))
        copies[2 + p].start()
    for copy in copies:
        copy.wait()


def exchange(blocks):
    return lax.all_to_all(blocks, "cand", split_axis=0, concat_axis=0, tiled=True)


def shards(cand_emb, cand_req, expert_ids, user_state, d_out, w_in, w_out):
    count, width = cand_emb.shape
    own = user_state.shape[0]
    experts = lax.axis_size("cand") * w_in.shape[0]
    capacity = 2 * count // experts
    chunks = width // LANES
    body = chunks * (2 * capacity + own)
    there = body + 8
    hbm = pl.BlockSpec(memory_space=pltpu.HBM)
    send, place = pl.pallas_call(
        functools.partial(pack_kernel, capacity),
        in_specs=[hbm] * 5,
        out_shape=(
            jax.ShapeDtypeStruct((experts, there, LANES), jnp.bfloat16),
            jax.ShapeDtypeStruct((1, count), jnp.float32),
        ),
        out_specs=(hbm, pl.BlockSpec(memory_space=pltpu.VMEM)),
        scratch_shapes=[
            pltpu.VMEM((1, count), jnp.int32),
            pltpu.VMEM((1, count), jnp.int32),
            pltpu.VMEM((count, width), jnp.bfloat16),
            pltpu.VMEM((count, width), jnp.bfloat16),
            pltpu.VMEM((own, width), jnp.bfloat16),
            pltpu.VMEM((experts, there, LANES), jnp.bfloat16),
            pltpu.SemaphoreType.DMA((5,)),
            pltpu.SemaphoreType.DMA((4,)),
        ],
        compiler_params=pltpu.CompilerParams(vmem_limit_bytes=60 * MIB),
        name="pack",
    )(expert_ids[None], cand_req[None], cand_emb, d_out, user_state)
    recv = exchange(send)
    send = pl.pallas_call(
        functools.partial(work_kernel, capacity, own),
        out_shape=jax.ShapeDtypeStruct((experts, body, LANES), jnp.bfloat16),
        compiler_params=pltpu.CompilerParams(vmem_limit_bytes=30 * MIB),
        name="work",
    )(recv, w_in[0], w_out[0])
    recv = exchange(send)
    outs = (
        jax.ShapeDtypeStruct((count, width), jnp.bfloat16),
        jax.ShapeDtypeStruct((count, width), jnp.bfloat16),
        jax.ShapeDtypeStruct((own, width), jnp.float32),
    )
    tower_out, cand_grad, user_grad = pl.pallas_call(
        functools.partial(unpack_kernel, capacity, own),
        out_shape=outs,
        out_specs=(hbm, hbm, hbm),
        scratch_shapes=[pltpu.VMEM(o.shape, o.dtype) for o in outs] + [pltpu.SemaphoreType.DMA((4,))],
        compiler_params=pltpu.CompilerParams(vmem_limit_bytes=24 * MIB),
        name="unpack",
    )(recv, place)
    return (tower_out, cand_grad, user_grad)


def solution(mesh):
    rows = P(("req", "cand"), None)
    ids = P(("req", "cand"))
    weights = P("cand", None, None)
    in_specs = (rows, ids, ids, rows, rows, weights, weights)
    return jax.shard_map(shards, mesh=mesh, in_specs=in_specs, out_specs=(rows, rows, rows), check_vma=False)
```

```python
import functools
import math

import jax
import jax.numpy as jnp
from jax import lax
from jax.experimental import pallas as pl
from jax.experimental.pallas import tpu as pltpu
from jax.sharding import PartitionSpec as P

US = 32
REQ_DEV = 8
LANES = 128
MIB = 1024 * 1024


def dot(a, b, dims=((1,), (0,))):
    return lax.dot_general(a, b, (dims, ((), ())), preferred_element_type=jnp.float32)


def iota(shape, dim):
    return lax.broadcasted_iota(jnp.int32, shape, dim)


def as_column(row):
    size = row.shape[1]
    eye = iota((size, size), 0) == iota((size, size), 1)
    return jnp.sum(jnp.where(eye, row, 0.0), axis=1, keepdims=True)


def read_rows(ref, first, count, width):
    blocks = ref.shape[0]
    chunks = [
        ref[:, first + c * count : first + (c + 1) * count, :].reshape(blocks * count, LANES)
        for c in range(width // LANES)
    ]
    return jnp.concatenate(chunks, axis=1)


def write_rows(ref, first, count, rows):
    blocks = ref.shape[0]
    for c in range(rows.shape[1] // LANES):
        ref[:, first + c * count : first + (c + 1) * count, :] = rows[:, c * LANES : (c + 1) * LANES].reshape(
            blocks, count, LANES
        )


def pack_kernel(
    capacity, ids_hbm, req_hbm, emb_hbm, grad_hbm, user_hbm, send_ref, place_ref,
    ids_ref, req_ref, emb_ref, grad_ref, user_ref, sems,
):
    pairs = (
        (ids_hbm, ids_ref), (req_hbm, req_ref), (user_hbm, user_ref), (emb_hbm, emb_ref), (grad_hbm, grad_ref),
    )
    copies = [pltpu.make_async_copy(src, dst, sems.at[i]) for i, (src, dst) in enumerate(pairs)]
    for copy in copies:
        copy.start()
    experts = send_ref.shape[0]
    count, width = emb_ref.shape
    chunks = width // LANES
    own = user_ref.shape[0]
    earlier = (iota((count, count), 0) < iota((count, count), 1)).astype(jnp.bfloat16)
    copies[0].wait()
    ids = ids_ref[...].astype(jnp.float32)
    named = (iota((experts, count), 0).astype(jnp.float32) == ids).astype(jnp.bfloat16)
    slot = jnp.sum(named.astype(jnp.float32) * dot(named, earlier), axis=0, keepdims=True)
    place = ids * capacity + slot
    place_ref[...] = as_column(place)
    copies[1].wait()
    copies[2].wait()
    first = 2 * chunks * capacity
    local_req = (req_ref[...] & (REQ_DEV - 1)).astype(jnp.float32)
    at_slot = iota((count, LANES), 1).astype(jnp.float32) == as_column(slot)
    requests = dot(named, jnp.where(at_slot, as_column(local_req), 0.0).astype(jnp.bfloat16))
    user = jnp.concatenate([user_ref[:, c * LANES : (c + 1) * LANES] for c in range(chunks)], axis=0)
    tail = send_ref.shape[1] - first
    user_tail = jnp.concatenate(
        [user.astype(jnp.float32), jnp.zeros((tail - chunks * own, LANES), jnp.float32)], axis=0
    )
    is_request = iota((experts, tail, LANES), 1) == chunks * own
    send_ref[:, first:, :] = jnp.where(is_request, requests[:, None, :], user_tail[None]).astype(jnp.bfloat16)
    copies[3].wait()
    copies[4].wait()
    spread = (iota((experts * capacity, count), 0).astype(jnp.float32) == place).astype(jnp.bfloat16)
    write_rows(send_ref, 0, capacity, dot(spread, emb_ref[...]).astype(jnp.bfloat16))
    write_rows(send_ref, chunks * capacity, capacity, dot(spread, grad_ref[...]).astype(jnp.bfloat16))


def work_kernel(capacity, own, recv_ref, w_in_ref, w_out_ref, send_ref):
    sources = recv_ref.shape[0]
    width = w_in_ref.shape[0]
    chunks = width // LANES
    count = sources * capacity
    scale = 1.0 / math.sqrt(width)
    emb = read_rows(recv_ref, 0, capacity, width)
    grad = read_rows(recv_ref, chunks * capacity, capacity, width)
    first = 2 * chunks * capacity
    keys_n = sources * own
    user_rows = chunks * own
    users = recv_ref[:, first : first + user_rows, :].astype(jnp.float32)
    keys = jnp.concatenate(
        [users[:, c * own : (c + 1) * own, :].reshape(keys_n, LANES) for c in range(chunks)], axis=1
    ).astype(jnp.bfloat16)
    requests = recv_ref[:, first + user_rows, :].astype(jnp.bfloat16)
    source_of = (iota((count, sources), 0) // capacity == iota((count, sources), 1)).astype(jnp.bfloat16)
    spread = dot(source_of, requests)
    mine = iota((count, LANES), 1) == iota((count, LANES), 0) % capacity
    request = jnp.sum(jnp.where(mine, spread, 0.0), axis=1, keepdims=True)
    member = (iota((count, keys_n), 1) // US).astype(jnp.float32) == request

    scores = dot(emb, keys, ((1,), (1,))) * scale
    peak = jnp.max(jnp.where(member, scores, -jnp.inf), axis=1, keepdims=True)
    weights = jnp.exp(jnp.where(member, scores - peak, -jnp.inf))
    probs = weights / jnp.sum(weights, axis=1, keepdims=True)
    probs_b = probs.astype(jnp.bfloat16)
    inputs = (emb.astype(jnp.float32) + dot(probs_b, keys)).astype(jnp.bfloat16)

    c0 = math.sqrt(2.0 / math.pi)
    outs, backs = [], []
    tile = count // 4
    for m in range(0, count, tile):
        pre = dot(inputs[m : m + tile], w_in_ref[...])
        back = dot(grad[m : m + tile], w_out_ref[...], ((1,), (1,)))
        square = pre * pre
        half = 0.5 + 0.5 * jnp.tanh(pre * (c0 + (c0 * 0.044715) * square))
        gelu = pre * half
        slope_g = half + gelu * (1.0 - half) * (2.0 * c0 + (6.0 * c0 * 0.044715) * square)
        outs.append(dot(gelu.astype(jnp.bfloat16), w_out_ref[...]).astype(jnp.bfloat16))
        backs.append(dot((back * slope_g).astype(jnp.bfloat16), w_in_ref[...], ((1,), (1,))).astype(jnp.bfloat16))
    write_rows(send_ref, 0, capacity, jnp.concatenate(outs, axis=0))
    d_in = jnp.concatenate(backs, axis=0)

    d_probs = dot(d_in, keys, ((1,), (1,)))
    center = jnp.sum(probs * d_probs, axis=1, keepdims=True)
    slope = (probs * (d_probs - center)).astype(jnp.bfloat16)
    cand_grad = d_in.astype(jnp.float32) + dot(slope, keys) * scale
    write_rows(send_ref, chunks * capacity, capacity, cand_grad.astype(jnp.bfloat16))
    share = dot(probs_b, d_in, ((0,), (0,))) + dot(slope, emb, ((0,), (0,))) * scale
    tail = jnp.concatenate(
        [share[:, c * LANES : (c + 1) * LANES].reshape(sources, own, LANES) for c in range(chunks)], axis=1
    )
    send_ref[:, first : first + user_rows, :] = tail.astype(jnp.bfloat16)


def unpack_kernel(capacity, own, recv_ref, place_ref, out_hbm, grad_hbm, user_hbm, out_ref, grad_ref, user_ref, sems):
    experts = recv_ref.shape[0]
    count, width = out_ref.shape
    chunks = width // LANES
    first = 2 * chunks * capacity
    total = jnp.sum(recv_ref[:, first:, :].astype(jnp.float32), axis=0)
    for c in range(chunks):
        user_ref[:, c * LANES : (c + 1) * LANES] = total[c * own : (c + 1) * own, :]
    copies = [pltpu.make_async_copy(user_ref, user_hbm, sems.at[0])]
    copies[0].start()
    pick = (iota((count, experts * capacity), 1).astype(jnp.float32) == place_ref[...]).astype(jnp.bfloat16)
    out_ref[...] = dot(pick, read_rows(recv_ref, 0, capacity, width)).astype(jnp.bfloat16)
    copies.append(pltpu.make_async_copy(out_ref, out_hbm, sems.at[1]))
    copies[1].start()
    grads = read_rows(recv_ref, chunks * capacity, capacity, width)
    part = count // 2
    for p in range(2):
        rows = pl.ds(p * part, part)
        grad_ref[rows, :] = dot(pick[p * part : (p + 1) * part], grads).astype(jnp.bfloat16)
        copies.append(pltpu.make_async_copy(grad_ref.at[rows, :], grad_hbm.at[rows, :], sems.at[2 + p]))
        copies[2 + p].start()
    for copy in copies:
        copy.wait()


def exchange(blocks):
    return lax.all_to_all(blocks, "cand", split_axis=0, concat_axis=0, tiled=True)


def shards(cand_emb, cand_req, expert_ids, user_state, d_out, w_in, w_out):
    count, width = cand_emb.shape
    own = user_state.shape[0]
    experts = lax.axis_size("cand") * w_in.shape[0]
    capacity = 2 * count // experts
    chunks = width // LANES
    body = chunks * (2 * capacity + own)
    there = body + 8
    hbm = pl.BlockSpec(memory_space=pltpu.HBM)
    send, place = pl.pallas_call(
        functools.partial(pack_kernel, capacity),
        in_specs=[hbm] * 5,
        out_shape=(
            pltpu.VMEM((experts, there, LANES), jnp.bfloat16),
            pltpu.VMEM((count, 1), jnp.float32),
        ),
        scratch_shapes=[
            pltpu.VMEM((1, count), jnp.int32),
            pltpu.VMEM((1, count), jnp.int32),
            pltpu.VMEM((count, width), jnp.bfloat16),
            pltpu.VMEM((count, width), jnp.bfloat16),
            pltpu.VMEM((own, width), jnp.bfloat16),
            pltpu.SemaphoreType.DMA((5,)),
        ],
        compiler_params=pltpu.CompilerParams(vmem_limit_bytes=56 * MIB),
        name="pack",
    )(expert_ids[None], cand_req[None], cand_emb, d_out, user_state)
    recv = exchange(send)
    send = pl.pallas_call(
        functools.partial(work_kernel, capacity, own),
        out_shape=jax.ShapeDtypeStruct((experts, body, LANES), jnp.bfloat16),
        compiler_params=pltpu.CompilerParams(vmem_limit_bytes=30 * MIB),
        name="work",
    )(recv, w_in[0], w_out[0])
    recv = exchange(send)
    outs = (
        jax.ShapeDtypeStruct((count, width), jnp.bfloat16),
        jax.ShapeDtypeStruct((count, width), jnp.bfloat16),
        jax.ShapeDtypeStruct((own, width), jnp.float32),
    )
    tower_out, cand_grad, user_grad = pl.pallas_call(
        functools.partial(unpack_kernel, capacity, own),
        out_shape=outs,
        out_specs=(hbm, hbm, hbm),
        scratch_shapes=[pltpu.VMEM(o.shape, o.dtype) for o in outs] + [pltpu.SemaphoreType.DMA((4,))],
        compiler_params=pltpu.CompilerParams(vmem_limit_bytes=24 * MIB),
        name="unpack",
    )(recv, place)
    return (tower_out, cand_grad, user_grad)


def solution(mesh):
    rows = P(("req", "cand"), None)
    ids = P(("req", "cand"))
    weights = P("cand", None, None)
    in_specs = (rows, ids, ids, rows, rows, weights, weights)
    return jax.shard_map(shards, mesh=mesh, in_specs=in_specs, out_specs=(rows, rows, rows), check_vma=False)
```

```python
import functools
import math

import jax
import jax.numpy as jnp
from jax import lax
from jax.experimental import pallas as pl
from jax.experimental.pallas import tpu as pltpu
from jax.sharding import PartitionSpec as P

US = 32
REQ_DEV = 8
LANES = 128
CORES = 2
MIB = 1024 * 1024


def dot(a, b, dims=((1,), (0,))):
    return lax.dot_general(a, b, (dims, ((), ())), preferred_element_type=jnp.float32)


def iota(shape, dim):
    return lax.broadcasted_iota(jnp.int32, shape, dim)


def as_column(row):
    size = row.shape[1]
    eye = iota((size, size), 0) == iota((size, size), 1)
    return jnp.sum(jnp.where(eye, row, 0.0), axis=1, keepdims=True)


def read_rows(ref, first, count, width):
    blocks = ref.shape[0]
    chunks = [
        ref[:, first + c * count : first + (c + 1) * count, :].reshape(blocks * count, LANES)
        for c in range(width // LANES)
    ]
    return jnp.concatenate(chunks, axis=1)


def write_rows(ref, first, count, rows):
    blocks = ref.shape[0]
    for c in range(rows.shape[1] // LANES):
        ref[:, first + c * count : first + (c + 1) * count, :] = rows[:, c * LANES : (c + 1) * LANES].reshape(
            blocks, count, LANES
        )


def pack_kernel(
    capacity, ids_hbm, req_hbm, emb_hbm, grad_hbm, user_hbm, send_ref, place_ref,
    ids_ref, req_ref, emb_ref, grad_ref, user_ref, sems,
):
    pairs = (
        (ids_hbm, ids_ref), (req_hbm, req_ref), (user_hbm, user_ref), (emb_hbm, emb_ref), (grad_hbm, grad_ref),
    )
    copies = [pltpu.make_async_copy(src, dst, sems.at[i]) for i, (src, dst) in enumerate(pairs)]
    for copy in copies:
        copy.start()
    experts = send_ref.shape[0]
    count, width = emb_ref.shape
    chunks = width // LANES
    own = user_ref.shape[0]
    earlier = (iota((count, count), 0) < iota((count, count), 1)).astype(jnp.bfloat16)
    copies[0].wait()
    ids = ids_ref[...].astype(jnp.float32)
    named = (iota((experts, count), 0).astype(jnp.float32) == ids).astype(jnp.bfloat16)
    slot = jnp.sum(named.astype(jnp.float32) * dot(named, earlier), axis=0, keepdims=True)
    place = ids * capacity + slot
    place_ref[...] = as_column(place)
    copies[1].wait()
    copies[2].wait()
    first = 2 * chunks * capacity
    local_req = (req_ref[...] & (REQ_DEV - 1)).astype(jnp.float32)
    at_slot = iota((count, LANES), 1).astype(jnp.float32) == as_column(slot)
    requests = dot(named, jnp.where(at_slot, as_column(local_req), 0.0).astype(jnp.bfloat16))
    tail = send_ref.shape[1] - first
    half = own // CORES
    tails = []
    for k in range(CORES):
        part = [user_ref[k * half : (k + 1) * half, c * LANES : (c + 1) * LANES] for c in range(chunks)]
        rest = jnp.zeros((tail - chunks * half, LANES), jnp.float32)
        tails.append(jnp.concatenate([p.astype(jnp.float32) for p in part] + [rest], axis=0))
    second = iota((experts, tail, LANES), 0) % CORES == 1
    user_tail = jnp.where(second, tails[1][None], tails[0][None])
    is_request = iota((experts, tail, LANES), 1) == chunks * half
    send_ref[:, first:, :] = jnp.where(is_request, requests[:, None, :], user_tail).astype(jnp.bfloat16)
    copies[3].wait()
    copies[4].wait()
    spread = (iota((experts * capacity, count), 0).astype(jnp.float32) == place).astype(jnp.bfloat16)
    write_rows(send_ref, 0, capacity, dot(spread, emb_ref[...]).astype(jnp.bfloat16))
    write_rows(send_ref, chunks * capacity, capacity, dot(spread, grad_ref[...]).astype(jnp.bfloat16))


def back_kernel(capacity, recv_ref, w_out_ref, back_ref, *half_ref):
    count = back_ref.shape[0]
    width = w_out_ref.shape[1]
    chunks = width // LANES
    start = 0 if half_ref else recv_ref.shape[0] - count // capacity
    if half_ref:
        first = 2 * chunks * capacity
        half_ref[0][...] = recv_ref[:, first : first + half_ref[0].shape[1], :]
    part = recv_ref.at[start : start + count // capacity]
    back_ref[...] = dot(read_rows(part, chunks * capacity, capacity, width), w_out_ref[...], ((1,), (1,)))


def work_kernel(capacity, own, recv_ref, other_ref, back1_ref, back2_ref, w_in_ref, w_out_ref, send_ref):
    sources = recv_ref.shape[0]
    width = w_in_ref.shape[0]
    chunks = width // LANES
    count = sources * capacity
    scale = 1.0 / math.sqrt(width)
    emb = read_rows(recv_ref, 0, capacity, width)
    first = 2 * chunks * capacity
    keys_n = sources * own
    half = own // CORES
    user_rows = chunks * own
    here = recv_ref[:, first : first + chunks * half, :].astype(jnp.float32)
    there = other_ref[...].astype(jnp.float32)
    low = lax.axis_index("cand") % CORES == 0
    keys = jnp.concatenate(
        [
            jnp.concatenate(
                [rows[:, c * half : (c + 1) * half, :].reshape(sources * half, LANES) for c in range(chunks)], axis=1
            )
            for rows in (jnp.where(low, here, there), jnp.where(low, there, here))
        ],
        axis=0,
    ).astype(jnp.bfloat16)
    requests = recv_ref[:, first + chunks * half, :].astype(jnp.bfloat16)
    source_of = (iota((count, sources), 0) // capacity == iota((count, sources), 1)).astype(jnp.bfloat16)
    spread = dot(source_of, requests)
    mine = iota((count, LANES), 1) == iota((count, LANES), 0) % capacity
    request = jnp.sum(jnp.where(mine, spread, 0.0), axis=1, keepdims=True)
    member = (iota((count, keys_n), 1) % (keys_n // CORES) // (US // CORES)).astype(jnp.float32) == request

    scores = dot(emb, keys, ((1,), (1,))) * scale
    peak = jnp.max(jnp.where(member, scores, -jnp.inf), axis=1, keepdims=True)
    weights = jnp.exp(jnp.where(member, scores - peak, -jnp.inf))
    probs = weights / jnp.sum(weights, axis=1, keepdims=True)
    probs_b = probs.astype(jnp.bfloat16)
    inputs = (emb.astype(jnp.float32) + dot(probs_b, keys)).astype(jnp.bfloat16)

    c0 = math.sqrt(2.0 / math.pi)
    outs, backs = [], []
    tile = count // 4
    for m in range(0, count, tile):
        pre = dot(inputs[m : m + tile], w_in_ref[...])
        back_ref, at = (back1_ref, m) if m < count // 2 else (back2_ref, m - count // 2)
        back = back_ref[at : at + tile, :]
        square = pre * pre
        upper = 0.5 + 0.5 * jnp.tanh(pre * (c0 + (c0 * 0.044715) * square))
        gelu = pre * upper
        slope_g = upper + gelu * (1.0 - upper) * (2.0 * c0 + (6.0 * c0 * 0.044715) * square)
        outs.append(dot(gelu.astype(jnp.bfloat16), w_out_ref[...]).astype(jnp.bfloat16))
        backs.append(dot((back * slope_g).astype(jnp.bfloat16), w_in_ref[...], ((1,), (1,))).astype(jnp.bfloat16))
    write_rows(send_ref, 0, capacity, jnp.concatenate(outs, axis=0))
    d_in = jnp.concatenate(backs, axis=0)

    d_probs = dot(d_in, keys, ((1,), (1,)))
    center = jnp.sum(probs * d_probs, axis=1, keepdims=True)
    slope = (probs * (d_probs - center)).astype(jnp.bfloat16)
    cand_grad = d_in.astype(jnp.float32) + dot(slope, keys) * scale
    write_rows(send_ref, chunks * capacity, capacity, cand_grad.astype(jnp.bfloat16))
    share = dot(probs_b, d_in, ((0,), (0,))) + dot(slope, emb, ((0,), (0,))) * scale
    part = keys_n // CORES
    tail = jnp.concatenate(
        [
            share[k * part : (k + 1) * part, c * LANES : (c + 1) * LANES].reshape(sources, half, LANES)
            for c in range(chunks)
            for k in range(CORES)
        ],
        axis=1,
    )
    send_ref[:, first : first + user_rows, :] = tail.astype(jnp.bfloat16)


def unpack_kernel(capacity, own, recv_ref, place_ref, out_hbm, grad_hbm, user_hbm, out_ref, grad_ref, user_ref, sems):
    experts = recv_ref.shape[0]
    count, width = out_ref.shape
    chunks = width // LANES
    first = 2 * chunks * capacity
    total = jnp.sum(recv_ref[:, first:, :].astype(jnp.float32), axis=0)
    for c in range(chunks):
        user_ref[:, c * LANES : (c + 1) * LANES] = total[c * own : (c + 1) * own, :]
    copies = [pltpu.make_async_copy(user_ref, user_hbm, sems.at[0])]
    copies[0].start()
    pick = (iota((count, experts * capacity), 1).astype(jnp.float32) == place_ref[...]).astype(jnp.bfloat16)
    part = count // 4
    for first_row, to_ref, to_hbm in ((0, out_ref, out_hbm), (chunks * capacity, grad_ref, grad_hbm)):
        values = read_rows(recv_ref, first_row, capacity, width)
        for p in range(4):
            rows = pl.ds(p * part, part)
            to_ref[rows, :] = dot(pick[p * part : (p + 1) * part], values).astype(jnp.bfloat16)
            copies.append(pltpu.make_async_copy(to_ref.at[rows, :], to_hbm.at[rows, :], sems.at[len(copies)]))
            copies[-1].start()
    for copy in copies:
        copy.wait()


def exchange(blocks):
    return lax.all_to_all(blocks, "cand", split_axis=0, concat_axis=0, tiled=True)


def shards(cand_emb, cand_req, expert_ids, user_state, d_out, w_in, w_out):
    count, width = cand_emb.shape
    own = user_state.shape[0]
    experts = lax.axis_size("cand") * w_in.shape[0]
    capacity = 2 * count // experts
    chunks = width // LANES
    body = chunks * (2 * capacity + own)
    there = 2 * chunks * capacity + 16
    hbm = pl.BlockSpec(memory_space=pltpu.HBM)
    send, place = pl.pallas_call(
        functools.partial(pack_kernel, capacity),
        in_specs=[hbm] * 5,
        out_shape=(
            pltpu.VMEM((experts, there, LANES), jnp.bfloat16),
            pltpu.VMEM((count, 1), jnp.float32),
        ),
        scratch_shapes=[
            pltpu.VMEM((1, count), jnp.int32),
            pltpu.VMEM((1, count), jnp.int32),
            pltpu.VMEM((count, width), jnp.bfloat16),
            pltpu.VMEM((count, width), jnp.bfloat16),
            pltpu.VMEM((own, width), jnp.bfloat16),
            pltpu.SemaphoreType.DMA((5,)),
        ],
        compiler_params=pltpu.CompilerParams(vmem_limit_bytes=56 * MIB),
        name="pack",
    )(expert_ids[None], cand_req[None], cand_emb, d_out, user_state)
    recv = exchange(send)
    slots = experts * capacity
    back_flops = slots * width * w_in.shape[2]
    half_rows = chunks * own // CORES

    def back(outs):
        return pl.pallas_call(
            functools.partial(back_kernel, capacity),
            out_shape=outs,
            compiler_params=pltpu.CompilerParams(vmem_limit_bytes=24 * MIB),
            cost_estimate=pl.CostEstimate(flops=back_flops, bytes_accessed=8 * MIB, transcendentals=0),
            name="back",
        )(recv, w_out[0])

    products = pltpu.VMEM((slots // 2, w_in.shape[2]), jnp.float32)
    back1, half = back((products, jax.ShapeDtypeStruct((experts, half_rows, LANES), jnp.bfloat16)))
    other = lax.ppermute(half, "cand", [(i, i ^ 1) for i in range(experts)])
    (back2,) = back((products,))
    send = pl.pallas_call(
        functools.partial(work_kernel, capacity, own),
        out_shape=jax.ShapeDtypeStruct((experts, body, LANES), jnp.bfloat16),
        compiler_params=pltpu.CompilerParams(vmem_limit_bytes=30 * MIB),
        name="work",
    )(recv, other, back1, back2, w_in[0], w_out[0])
    recv = exchange(send)
    outs = (
        jax.ShapeDtypeStruct((count, width), jnp.bfloat16),
        jax.ShapeDtypeStruct((count, width), jnp.bfloat16),
        jax.ShapeDtypeStruct((own, width), jnp.float32),
    )
    tower_out, cand_grad, user_grad = pl.pallas_call(
        functools.partial(unpack_kernel, capacity, own),
        out_shape=outs,
        out_specs=(hbm, hbm, hbm),
        scratch_shapes=[pltpu.VMEM(o.shape, o.dtype) for o in outs] + [pltpu.SemaphoreType.DMA((9,))],
        compiler_params=pltpu.CompilerParams(vmem_limit_bytes=24 * MIB),
        name="unpack",
    )(recv, place)
    return (tower_out, cand_grad, user_grad)


def solution(mesh):
    rows = P(("req", "cand"), None)
    ids = P(("req", "cand"))
    weights = P("cand", None, None)
    in_specs = (rows, ids, ids, rows, rows, weights, weights)
    return jax.shard_map(shards, mesh=mesh, in_specs=in_specs, out_specs=(rows, rows, rows), check_vma=False)
```

```python
import functools
import math

import jax
import jax.numpy as jnp
from jax import lax
from jax.experimental import pallas as pl
from jax.experimental.pallas import tpu as pltpu
from jax.sharding import PartitionSpec as P

US = 32
REQ_DEV = 8
LANES = 128
CORES = 2
MIB = 1024 * 1024


def dot(a, b, dims=((1,), (0,))):
    return lax.dot_general(a, b, (dims, ((), ())), preferred_element_type=jnp.float32)


def iota(shape, dim):
    return lax.broadcasted_iota(jnp.int32, shape, dim)


def as_column(row):
    size = row.shape[1]
    eye = iota((size, size), 0) == iota((size, size), 1)
    return jnp.sum(jnp.where(eye, row, 0.0), axis=1, keepdims=True)


def read_rows(ref, first, count, width):
    blocks = ref.shape[0]
    chunks = [
        ref[:, first + c * count : first + (c + 1) * count, :].reshape(blocks * count, LANES)
        for c in range(width // LANES)
    ]
    return jnp.concatenate(chunks, axis=1)


def write_rows(ref, first, count, rows):
    blocks = ref.shape[0]
    for c in range(rows.shape[1] // LANES):
        ref[:, first + c * count : first + (c + 1) * count, :] = rows[:, c * LANES : (c + 1) * LANES].reshape(
            blocks, count, LANES
        )


def pack_kernel(
    capacity, ids_hbm, req_hbm, emb_hbm, grad_hbm, user_hbm, send_ref, place_ref,
    ids_ref, req_ref, emb_ref, grad_ref, user_ref, sems,
):
    pairs = (
        (ids_hbm, ids_ref), (req_hbm, req_ref), (user_hbm, user_ref), (emb_hbm, emb_ref), (grad_hbm, grad_ref),
    )
    copies = [pltpu.make_async_copy(src, dst, sems.at[i]) for i, (src, dst) in enumerate(pairs)]
    for copy in copies:
        copy.start()
    experts = send_ref.shape[0]
    count, width = emb_ref.shape
    chunks = width // LANES
    own = user_ref.shape[0]
    earlier = (iota((count, count), 0) < iota((count, count), 1)).astype(jnp.bfloat16)
    copies[0].wait()
    ids = ids_ref[...].astype(jnp.float32)
    named = (iota((experts, count), 0).astype(jnp.float32) == ids).astype(jnp.bfloat16)
    slot = jnp.sum(named.astype(jnp.float32) * dot(named, earlier), axis=0, keepdims=True)
    place = ids * capacity + slot
    place_ref[...] = as_column(place)
    copies[1].wait()
    copies[2].wait()
    first = 2 * chunks * capacity
    local_req = (req_ref[...] & (REQ_DEV - 1)).astype(jnp.float32)
    at_slot = iota((count, LANES), 1).astype(jnp.float32) == as_column(slot)
    requests = dot(named, jnp.where(at_slot, as_column(local_req), 0.0).astype(jnp.bfloat16))
    tail = send_ref.shape[1] - first
    half = own // CORES
    tails = []
    for k in range(CORES):
        part = [user_ref[k * half : (k + 1) * half, c * LANES : (c + 1) * LANES] for c in range(chunks)]
        rest = jnp.zeros((tail - chunks * half, LANES), jnp.float32)
        tails.append(jnp.concatenate([p.astype(jnp.float32) for p in part] + [rest], axis=0))
    second = iota((experts, tail, LANES), 0) % CORES == 1
    user_tail = jnp.where(second, tails[1][None], tails[0][None])
    is_request = iota((experts, tail, LANES), 1) == chunks * half
    send_ref[:, first:, :] = jnp.where(is_request, requests[:, None, :], user_tail).astype(jnp.bfloat16)
    copies[3].wait()
    copies[4].wait()
    spread = (iota((experts * capacity, count), 0).astype(jnp.float32) == place).astype(jnp.bfloat16)
    write_rows(send_ref, 0, capacity, dot(spread, emb_ref[...]).astype(jnp.bfloat16))
    write_rows(send_ref, chunks * capacity, capacity, dot(spread, grad_ref[...]).astype(jnp.bfloat16))


def back_kernel(capacity, recv_ref, w_out_ref, back_ref, *half_ref):
    count = back_ref.shape[0]
    width = w_out_ref.shape[1]
    chunks = width // LANES
    start = 0 if half_ref else recv_ref.shape[0] // 4
    if half_ref:
        first = 2 * chunks * capacity
        half_ref[0][...] = recv_ref[:, first : first + half_ref[0].shape[1], :]
    part = recv_ref.at[start : start + count // capacity]
    back_ref[...] = dot(read_rows(part, chunks * capacity, capacity, width), w_out_ref[...], ((1,), (1,)))


def work_kernel(capacity, own, recv_ref, other_ref, back1_ref, back2_ref, w_in_ref, w_out_ref, send_ref):
    sources = recv_ref.shape[0]
    width = w_in_ref.shape[0]
    chunks = width // LANES
    count = sources * capacity
    scale = 1.0 / math.sqrt(width)
    emb = read_rows(recv_ref, 0, capacity, width)
    last = recv_ref.at[sources - sources // 4 :]
    grad = read_rows(last, chunks * capacity, capacity, width)
    first = 2 * chunks * capacity
    keys_n = sources * own
    half = own // CORES
    user_rows = chunks * own
    here = recv_ref[:, first : first + chunks * half, :].astype(jnp.float32)
    there = other_ref[...].astype(jnp.float32)
    low = lax.axis_index("cand") % CORES == 0
    keys = jnp.concatenate(
        [
            jnp.concatenate(
                [rows[:, c * half : (c + 1) * half, :].reshape(sources * half, LANES) for c in range(chunks)], axis=1
            )
            for rows in (jnp.where(low, here, there), jnp.where(low, there, here))
        ],
        axis=0,
    ).astype(jnp.bfloat16)
    requests = recv_ref[:, first + chunks * half, :].astype(jnp.bfloat16)
    source_of = (iota((count, sources), 0) // capacity == iota((count, sources), 1)).astype(jnp.bfloat16)
    spread = dot(source_of, requests)
    mine = iota((count, LANES), 1) == iota((count, LANES), 0) % capacity
    request = jnp.sum(jnp.where(mine, spread, 0.0), axis=1, keepdims=True)
    member = (iota((count, keys_n), 1) % (keys_n // CORES) // (US // CORES)).astype(jnp.float32) == request

    scores = dot(emb, keys, ((1,), (1,))) * scale
    peak = jnp.max(jnp.where(member, scores, -jnp.inf), axis=1, keepdims=True)
    weights = jnp.exp(jnp.where(member, scores - peak, -jnp.inf))
    probs = weights / jnp.sum(weights, axis=1, keepdims=True)
    probs_b = probs.astype(jnp.bfloat16)
    inputs = (emb.astype(jnp.float32) + dot(probs_b, keys)).astype(jnp.bfloat16)

    c0 = math.sqrt(2.0 / math.pi)
    outs, backs = [], []
    tile = count // 4
    for m in range(0, count, tile):
        pre = dot(inputs[m : m + tile], w_in_ref[...])
        if m < tile:
            back = back1_ref[...]
        elif m < 3 * tile:
            back = back2_ref[m - tile : m, :]
        else:
            back = dot(grad, w_out_ref[...], ((1,), (1,)))
        square = pre * pre
        upper = 0.5 + 0.5 * jnp.tanh(pre * (c0 + (c0 * 0.044715) * square))
        gelu = pre * upper
        slope_g = upper + gelu * (1.0 - upper) * (2.0 * c0 + (6.0 * c0 * 0.044715) * square)
        outs.append(dot(gelu.astype(jnp.bfloat16), w_out_ref[...]).astype(jnp.bfloat16))
        backs.append(dot((back * slope_g).astype(jnp.bfloat16), w_in_ref[...], ((1,), (1,))).astype(jnp.bfloat16))
    write_rows(send_ref, 0, capacity, jnp.concatenate(outs, axis=0))
    d_in = jnp.concatenate(backs, axis=0)

    d_probs = dot(d_in, keys, ((1,), (1,)))
    center = jnp.sum(probs * d_probs, axis=1, keepdims=True)
    slope = (probs * (d_probs - center)).astype(jnp.bfloat16)
    cand_grad = d_in.astype(jnp.float32) + dot(slope, keys) * scale
    write_rows(send_ref, chunks * capacity, capacity, cand_grad.astype(jnp.bfloat16))
    share = dot(probs_b, d_in, ((0,), (0,))) + dot(slope, emb, ((0,), (0,))) * scale
    part = keys_n // CORES
    tail = jnp.concatenate(
        [
            share[k * part : (k + 1) * part, c * LANES : (c + 1) * LANES].reshape(sources, half, LANES)
            for c in range(chunks)
            for k in range(CORES)
        ],
        axis=1,
    )
    send_ref[:, first : first + user_rows, :] = tail.astype(jnp.bfloat16)


def unpack_kernel(capacity, own, recv_ref, place_ref, out_hbm, grad_hbm, user_hbm, out_ref, grad_ref, user_ref, sems):
    experts = recv_ref.shape[0]
    count, width = out_ref.shape
    chunks = width // LANES
    first = 2 * chunks * capacity
    total = jnp.sum(recv_ref[:, first:, :].astype(jnp.float32), axis=0)
    for c in range(chunks):
        user_ref[:, c * LANES : (c + 1) * LANES] = total[c * own : (c + 1) * own, :]
    copies = [pltpu.make_async_copy(user_ref, user_hbm, sems.at[0])]
    copies[0].start()
    pick = (iota((count, experts * capacity), 1).astype(jnp.float32) == place_ref[...]).astype(jnp.bfloat16)
    part = count // 4
    for first_row, to_ref, to_hbm in ((0, out_ref, out_hbm), (chunks * capacity, grad_ref, grad_hbm)):
        values = read_rows(recv_ref, first_row, capacity, width)
        for p in range(4):
            rows = pl.ds(p * part, part)
            to_ref[rows, :] = dot(pick[p * part : (p + 1) * part], values).astype(jnp.bfloat16)
            copies.append(pltpu.make_async_copy(to_ref.at[rows, :], to_hbm.at[rows, :], sems.at[len(copies)]))
            copies[-1].start()
    for copy in copies:
        copy.wait()


def exchange(blocks):
    return lax.all_to_all(blocks, "cand", split_axis=0, concat_axis=0, tiled=True)


def shards(cand_emb, cand_req, expert_ids, user_state, d_out, w_in, w_out):
    count, width = cand_emb.shape
    own = user_state.shape[0]
    experts = lax.axis_size("cand") * w_in.shape[0]
    capacity = 2 * count // experts
    chunks = width // LANES
    body = chunks * (2 * capacity + own)
    there = 2 * chunks * capacity + 16
    hbm = pl.BlockSpec(memory_space=pltpu.HBM)
    send, place = pl.pallas_call(
        functools.partial(pack_kernel, capacity),
        in_specs=[hbm] * 5,
        out_shape=(
            pltpu.VMEM((experts, there, LANES), jnp.bfloat16),
            pltpu.VMEM((count, 1), jnp.float32),
        ),
        scratch_shapes=[
            pltpu.VMEM((1, count), jnp.int32),
            pltpu.VMEM((1, count), jnp.int32),
            pltpu.VMEM((count, width), jnp.bfloat16),
            pltpu.VMEM((count, width), jnp.bfloat16),
            pltpu.VMEM((own, width), jnp.bfloat16),
            pltpu.SemaphoreType.DMA((5,)),
        ],
        compiler_params=pltpu.CompilerParams(vmem_limit_bytes=56 * MIB),
        name="pack",
    )(expert_ids[None], cand_req[None], cand_emb, d_out, user_state)
    recv = exchange(send)
    slots = experts * capacity
    back_flops = slots * width * w_in.shape[2]
    half_rows = chunks * own // CORES

    def back(outs):
        return pl.pallas_call(
            functools.partial(back_kernel, capacity),
            out_shape=outs,
            compiler_params=pltpu.CompilerParams(vmem_limit_bytes=24 * MIB),
            cost_estimate=pl.CostEstimate(flops=back_flops, bytes_accessed=8 * MIB, transcendentals=0),
            name="back",
        )(recv, w_out[0])

    back1, half = back((pltpu.VMEM((slots // 4, w_in.shape[2]), jnp.float32), jax.ShapeDtypeStruct((experts, half_rows, LANES), jnp.bfloat16)))
    other = lax.ppermute(half, "cand", [(i, i ^ 1) for i in range(experts)])
    (back2,) = back((pltpu.VMEM((slots // 2, w_in.shape[2]), jnp.float32),))
    send = pl.pallas_call(
        functools.partial(work_kernel, capacity, own),
        out_shape=jax.ShapeDtypeStruct((experts, body, LANES), jnp.bfloat16),
        compiler_params=pltpu.CompilerParams(vmem_limit_bytes=30 * MIB),
        name="work",
    )(recv, other, back1, back2, w_in[0], w_out[0])
    recv = exchange(send)
    outs = (
        jax.ShapeDtypeStruct((count, width), jnp.bfloat16),
        jax.ShapeDtypeStruct((count, width), jnp.bfloat16),
        jax.ShapeDtypeStruct((own, width), jnp.float32),
    )
    tower_out, cand_grad, user_grad = pl.pallas_call(
        functools.partial(unpack_kernel, capacity, own),
        out_shape=outs,
        out_specs=(hbm, hbm, hbm),
        scratch_shapes=[pltpu.VMEM(o.shape, o.dtype) for o in outs] + [pltpu.SemaphoreType.DMA((9,))],
        compiler_params=pltpu.CompilerParams(vmem_limit_bytes=24 * MIB),
        name="unpack",
    )(recv, place)
    return (tower_out, cand_grad, user_grad)


def solution(mesh):
    rows = P(("req", "cand"), None)
    ids = P(("req", "cand"))
    weights = P("cand", None, None)
    in_specs = (rows, ids, ids, rows, rows, weights, weights)
    return jax.shard_map(shards, mesh=mesh, in_specs=in_specs, out_specs=(rows, rows, rows), check_vma=False)
```
